32 devices in a mesh: gx: 8 (over z, y), gy: 4 (over x, core).
Axes of the slice: x: 2, y: 2, z: 4, core: 2. Of those that a mesh axis runs over, the one named last changes fastest.
Arguments:
- features: bfloat16 [64, 8, 8, 8, 256], P(('gx', 'gy')), may hold values from -6 to 6
- cotangent: bfloat16 [64, 8, 8, 8, 256], P(('gx', 'gy')), may hold values from -6 to 6
- kernel: bfloat16 [27, 256, 256], replicated, may hold values from -0.078125 to 0.078125
- occupancy: int32 [64, 512], P(('gx', 'gy')), may hold values 0 or 1
- neighbors: int32 [64, 27], P(('gx', 'gy')), may hold values from -1 to 1, as said below
Outputs:
- out_features: bfloat16 [64, 8, 8, 8, 256], P(('gx', 'gy'))
- in_grad: bfloat16 [64, 8, 8, 8, 256], P(('gx', 'gy'))
- kernel_grad: float32 [27, 256, 256], replicated
The draws below stay inside these ranges and needn't reach their ends.
Inputs may be any that keep to these rules, and one draw needn't show every extreme that they name: neighbors[b, k] is the slot of the occupied brick at level L + oz in column (cx + ox, cy + oy), where L is brick b's level, and -1 where that column lies outside the 8 x 4 grid or that brick is not occupied; each column holds 2 occupied bricks among 4 levels, slots in rising level; the offset k = 13 entry of a brick is its own slot.
All inputs are finite; a program needn't handle non-finite values. No bound on the sum of `occupancy` on one device may be relied on, other than what follows from the above.
Results may differ from the reference program's by a relative error of at most 0.001.
Values may be sent and summed in bfloat16 or wider, within the bound.
A program may use at most 128 MiB of HBM per device.

```python
import jax
import jax.numpy as jnp
from jax import lax

C = 256
KOFF = 27
BRICKS_DEV = 2
LEVELS = 4
COLS_X = 8
COLS_Y = 4
BRICKS = 64


def draw_neighbors(key, part):
    key = jax.random.fold_in(key, 7)
    scores = jax.random.randint(key, (COLS_X, COLS_Y, LEVELS), 0, 1 << 20) * LEVELS + jnp.arange(LEVELS, dtype=jnp.int32)
    chosen = jnp.sort(lax.top_k(scores, BRICKS_DEV)[1].astype(jnp.int32), axis=-1)
    hits = (chosen[:, :, :, None] == jnp.arange(LEVELS, dtype=jnp.int32)).astype(jnp.int32)
    slot_of = jnp.where(jnp.sum(hits, axis=2) > 0, jnp.sum(hits * jnp.arange(BRICKS_DEV, dtype=jnp.int32)[:, None], axis=2), -1)
    table = jnp.pad(slot_of, ((1, 1), (1, 1), (1, 1)), constant_values=-1)
    col_x = jnp.arange(COLS_X, dtype=jnp.int32)[:, None, None]
    col_y = jnp.arange(COLS_Y, dtype=jnp.int32)[None, :, None]
    entries = []
    for ox in (-1, 0, 1):
        for oy in (-1, 0, 1):
            for oz in (-1, 0, 1):
                entries.append(table[col_x + 1 + ox, col_y + 1 + oy, chosen + 1 + oz])
    return jnp.stack(entries, -1).reshape(BRICKS, KOFF).astype(jnp.int32)


def touch_ends(array, stream_key, least, top_value):
    longest = array.shape.index(max(array.shape))
    spots = []
    for shift in (0, 1):
        where = [jax.random.randint(jax.random.fold_in(stream_key, axis), (), 0, length) for axis, length in enumerate(array.shape)]
        where[longest] = (where[longest] + shift) % array.shape[longest]
        spots.append(tuple(where))
    return array.at[spots[0]].set(least).at[spots[1]].set(top_value)


def steps_of(stream_key, dims, cuts, least, high):
    def one(dim, shards_of):
        draws = jax.random.uniform(jax.random.fold_in(jax.random.fold_in(stream_key, 6), dim), (shards_of,), jnp.float32, least / len(cuts), high / len(cuts))
        return jnp.repeat(jnp.exp(draws), dims[dim] // shards_of).reshape((-1,) + (1,) * (len(dims) - dim - 1))

    gain = one(*cuts[0])
    for cut in cuts[1:]:
        gain = gain * one(*cut)
    return gain


def gaussian(rng, shape, spread, limit, split=(), kind=jnp.bfloat16):
    loudness = steps_of(rng, shape, split, -0.22, 0.18) if split else 1.0
    values = jax.random.normal(rng, shape, jnp.float32) * spread * loudness
    return jnp.minimum(jnp.maximum(values, -limit), limit).astype(kind)


def setup_inputs(seed: int = 0) -> dict:
    keys = jax.random.split(jax.random.key(seed), 6)
    features = gaussian(keys[0], (BRICKS, 8, 8, 8, C), 1.0, 6.0, ((0, 32),))
    cotangent = gaussian(keys[1], (BRICKS, 8, 8, 8, C), 1.0, 6.0, ((0, 32),))
    kernel = gaussian(keys[2], (KOFF, C, C), (KOFF * C) ** -0.5, 0.078125)
    occupancy = touch_ends((jax.random.randint(keys[3], (BRICKS, 512), 0, 4) < 3).astype(jnp.int32), jax.random.fold_in(keys[3], 1), 0, 1)
    neighbors = draw_neighbors(jax.random.fold_in(keys[5], 71), 0)
    return dict(features=features, cotangent=cotangent, kernel=kernel, occupancy=occupancy, neighbors=neighbors)


layer_pick = {-1: slice(7, 8), 0: slice(0, 8), 1: slice(0, 1)}


def gather_grid(field, neighbors):
    zero = jnp.zeros((1,) + field.shape[1:], field.dtype)
    source = jnp.concatenate([field, zero], 0)
    ids = jnp.arange(BRICKS, dtype=jnp.int32)
    column = ids // BRICKS_DEV
    col_x = column // COLS_Y
    col_y = column % COLS_Y
    x_parts = []
    for ox in (-1, 0, 1):
        y_parts = []
        for oy in (-1, 0, 1):
            z_parts = []
            for oz in (-1, 0, 1):
                offset = 9 * (ox + 1) + 3 * (oy + 1) + (oz + 1)
                slot = neighbors[:, offset].astype(jnp.int32)
                target = ((col_x + ox) * COLS_Y + col_y + oy) * BRICKS_DEV + slot
                target = jnp.where(slot >= 0, target, BRICKS).astype(jnp.int32)
                piece = source[:, layer_pick[ox], layer_pick[oy], layer_pick[oz]]
                z_parts.append(jnp.take(piece, target, axis=0))
            y_parts.append(jnp.concatenate(z_parts, 3))
        x_parts.append(jnp.concatenate(y_parts, 2))
    return jnp.concatenate(x_parts, 1)


def reference(features, cotangent, kernel, occupancy, neighbors):
    mask_b = occupancy.reshape(BRICKS, 8, 8, 8, 1).astype(jnp.bfloat16)
    mask_f = occupancy.reshape(BRICKS * 512, 1).astype(jnp.float32)
    masked = features * mask_b
    masked_grad = cotangent * mask_b
    padded_in = gather_grid(masked, neighbors)
    padded_grad = gather_grid(masked_grad, neighbors)
    flat_grad = masked_grad.reshape(-1, C)
    forward = jnp.zeros((BRICKS * 512, C), jnp.float32)
    backward = jnp.zeros((BRICKS * 512, C), jnp.float32)
    grads = []
    for step_x in range(3):
        for step_y in range(3):
            for step_z in range(3):
                offset = 9 * step_x + 3 * step_y + step_z
                window = padded_in[:, step_x:step_x + 8, step_y:step_y + 8, step_z:step_z + 8].reshape(-1, C)
                forward = forward + jnp.dot(window, kernel[offset], preferred_element_type=jnp.float32)
                grads.append(lax.dot_general(window, flat_grad, (((0,), (0,)), ((), ())), preferred_element_type=jnp.float32))
                back_window = padded_grad[:, 2 - step_x:10 - step_x, 2 - step_y:10 - step_y, 2 - step_z:10 - step_z].reshape(-1, C)
                backward = backward + lax.dot_general(back_window, kernel[offset], (((1,), (1,)), ((), ())), preferred_element_type=jnp.float32)
    out_features = (forward * mask_f).astype(jnp.bfloat16).reshape(BRICKS, 8, 8, 8, C)
    in_grad = (backward * mask_f).astype(jnp.bfloat16).reshape(BRICKS, 8, 8, 8, C)
    kernel_grad = jnp.stack(grads) * jnp.float32(1.0 / (512.0 * BRICKS) ** 0.5)
    return out_features, in_grad, kernel_grad
```

```python
import functools

import jax
import jax.numpy as jnp
from jax import lax
from jax.experimental import pallas as pl
from jax.experimental.pallas import tpu as pltpu
from jax.sharding import PartitionSpec as P

MESH = pl.DeviceIdType.MESH
VMEM = pltpu.VMEM
PARTS = 3
LANES = 128


def shift_by_one(cells, axis):
    count = lax.axis_size(axis)
    ends = count - 1
    head = lambda dim: lax.slice_in_dim(cells, 0, 1, axis=dim)
    tail = lambda dim: lax.slice_in_dim(cells, cells.shape[dim] - 1, cells.shape[dim], axis=dim)
    up = [(i, i + 1) for i in range(ends)]
    down = [(i + 1, i) for i in range(ends)]
    return lambda dim: jnp.concatenate(
        [lax.ppermute(tail(dim), axis, up), cells, lax.ppermute(head(dim), axis, down)], axis=dim
    )


def spread(table, dim):
    first = lax.slice_in_dim(table, 0, 1, axis=dim)
    middle = lax.slice_in_dim(table, 1, 2, axis=dim)
    last = lax.slice_in_dim(table, 2, 3, axis=dim)
    return jnp.concatenate([first] + [middle] * 8 + [last], axis=dim)


def z_shifted(both, neighbors):
    slots = both.shape[1]
    wide = shift_by_one(both, "gx")(2)
    wide = shift_by_one(wide, "gy")(3)
    table = spread(spread(neighbors.reshape(slots, 3, 3, 3), 1), 2)

    def pick(layer, oz):
        total = None
        for slot in range(slots):
            hit = (table[:, :, :, oz] == slot)[None, :, :, :, None, None]
            part = jnp.where(hit, wide[:, slot : slot + 1, :, :, layer], jnp.zeros((), wide.dtype))
            total = part if total is None else total + part
        return total

    low = pick(slice(7, 8), 0)
    mid = pick(slice(0, 8), 1)
    high = pick(slice(0, 1), 2)
    return jnp.stack(
        [
            jnp.concatenate([low, mid[..., :7, :]], 4),
            mid,
            jnp.concatenate([mid[..., 1:, :], high], 4),
        ]
    )


def conv_kernel(slots, even_ref, odd_ref, w_ref, wt_ref, grad_t_ref, mask_ref, out_ref, back_ref, terms_ref, acc_f, acc_b):
    ox = pl.program_id(0)

    def window(tensor, brick, oy, oz):
        if oy == 1:
            value = odd_ref[oz, tensor, brick, pl.ds(ox, 8)]
        else:
            value = even_ref[oz, tensor, brick, pl.ds(ox, 8), 8 * oy : 8 * oy + 64]
        return value.reshape(512, value.shape[-1])

    for oy in range(3):
        weights = w_ref[3 * oy : 3 * oy + 3].reshape(-1, w_ref.shape[-1])
        weights_t = wt_ref[3 * oy : 3 * oy + 3].reshape(-1, wt_ref.shape[-1])
        for brick in range(slots):
            rows = slice(512 * brick, 512 * brick + 512)
            for tensor, acc, rhs in ((0, acc_f, weights), (1, acc_b, weights_t)):
                lhs = jnp.concatenate([window(tensor, brick, oy, oz) for oz in range(3)], 1)
                part = jnp.dot(lhs, rhs, preferred_element_type=jnp.float32)
                if oy == 0:
                    @pl.when(ox == 0)
                    def _():
                        acc[rows] = part

                    @pl.when(ox != 0)
                    def _():
                        acc[rows] += part
                else:
                    acc[rows] += part
        for oz in range(3):
            both = jnp.concatenate([window(0, brick, oy, oz) for brick in range(slots)], 0)
            term = jnp.dot(grad_t_ref[...], both, preferred_element_type=jnp.float32)
            terms_ref[3 * oy + oz] = term.T

    @pl.when(ox == 2)
    def _():
        out_ref[...] = (acc_f[...] * mask_ref[...]).astype(out_ref.dtype)
        back_ref[...] = (acc_b[...] * mask_ref[...]).astype(back_ref.dtype)


def conv(even, odd, weights, weights_t, grad_t, mask):
    slots = even.shape[2]
    width = even.shape[-1]
    rows = slots * 512
    whole = lambda array: pl.BlockSpec(array.shape, lambda i: (0,) * array.ndim)
    nine = pl.BlockSpec((9, width, width), lambda i: (i, 0, 0))
    flat = pl.BlockSpec((rows, width), lambda i: (0, 0))
    return pl.pallas_call(
        functools.partial(conv_kernel, slots),
        grid=(3,),
        in_specs=[whole(even), whole(odd), nine, nine, whole(grad_t), whole(mask)],
        out_specs=[flat, flat, nine],
        out_shape=[
            jax.ShapeDtypeStruct((rows, width), jnp.bfloat16),
            jax.ShapeDtypeStruct((rows, width), jnp.bfloat16),
            jax.ShapeDtypeStruct((27, width, width), jnp.float32),
        ],
        scratch_shapes=[VMEM((rows, width), jnp.float32), VMEM((rows, width), jnp.float32)],
        compiler_params=pltpu.CompilerParams(
            dimension_semantics=("arbitrary",), vmem_limit_bytes=56 * 2**20
        ),
        cost_estimate=pl.CostEstimate(
            flops=27 * 6 * rows * width * width, bytes_accessed=24 * 2**20, transcendentals=0
        ),
    )(even, odd, weights, weights_t, grad_t, mask)


def reduce_kernel(pair, orders, scale, terms_ref, out_ref, acc, *rest):
    stages = len(orders[0]) + 1
    recv, (send_sem, recv_sem) = rest[:stages], rest[stages:]
    part_rows = acc.shape[1]
    place = {"gx": lax.axis_index("gx"), "gy": lax.axis_index("gy")}

    def bit_of(bit):
        axis, step = bit
        return (place[axis] // step) % 2

    def partner(bit):
        axis, step = bit
        there = dict(place)
        there[axis] = place[axis] + step - 2 * step * bit_of(bit)
        return (there["gx"], there["gy"])

    barrier = pltpu.get_barrier_semaphore()
    for bit in [pair] + sorted(orders[0]):
        pl.semaphore_signal(barrier, inc=1, device_id=partner(bit), device_id_type=MESH)
    pl.semaphore_wait(barrier, stages)

    side = bit_of(pair)
    mine = pl.ds(pl.multiple_of(side * LANES, LANES), LANES)
    other = pl.ds(pl.multiple_of((1 - side) * LANES, LANES), LANES)
    started = []

    def send(src, dst, step, part, bit):
        copy = pltpu.make_async_remote_copy(
            src_ref=src,
            dst_ref=dst,
            send_sem=send_sem.at[step, part],
            recv_sem=recv_sem.at[step, part],
            device_id=partner(bit),
            device_id_type=MESH,
        )
        copy.start()
        started.append(copy)
        return copy

    base = [0] * PARTS
    flying = [
        send(terms_ref.at[pl.ds(p * part_rows, part_rows), other], recv[0].at[p], 0, p, pair)
        for p in range(PARTS)
    ]
    for stage in range(stages):
        size = part_rows >> stage
        half = size // 2
        block = min(size, 144)
        for p in range(PARTS):
            flying[p].wait_recv()

            @pl.loop(0, size // block)
            def _(i):
                here = pl.ds(pl.multiple_of(i * block, 16), block)
                there = pl.ds(pl.multiple_of(base[p] + i * block, 16), block)
                if stage == 0:
                    there_in = pl.ds(pl.multiple_of(p * part_rows + i * block, 16), block)
                    acc[p, here] = terms_ref[there_in, mine] + recv[0][p, here]
                else:
                    acc[p, there] = acc[p, there] + recv[stage][p, here]

            if stage < stages - 1:
                bit = orders[p][stage]
                away = pl.multiple_of(base[p] + (1 - bit_of(bit)) * half, 16)
                base[p] = base[p] + bit_of(bit) * half
                flying[p] = send(acc.at[p, pl.ds(away, half)], recv[stage + 1].at[p], stage + 1, p, bit)
            else:
                own = pl.ds(pl.multiple_of(base[p], 16), size)
                full = pl.ds(pl.multiple_of(p * part_rows + base[p], 16), size)
                out_ref[full, mine] = acc[p, own] * scale
                span = out_ref.at[full, mine]
                flying[p] = send(span, span, stages, p, orders[p][-1])
    for back in range(1, stages + 1):
        level = stages - 1 - back
        size = part_rows >> level if level >= 0 else 0
        for p in range(PARTS):
            flying[p].wait_recv()
            if level < 0:
                continue
            base[p] = base[p] - bit_of(orders[p][level]) * (size // 2)
            full = pl.ds(pl.multiple_of(p * part_rows + base[p], 16), size)
            span = out_ref.at[full, mine]
            flying[p] = send(span, span, stages + back, p, orders[p][level - 1] if level > 0 else pair)
    for copy in started:
        copy.wait_send()


def sum_plan(mesh, rows):
    sizes = dict(mesh.shape)
    if sizes["gx"] != 8 or sizes["gy"] != 4 or rows % (PARTS * 16 * 16):
        return None
    pair, x, y, z_near, z_far = ("gy", 1), ("gy", 2), ("gx", 1), ("gx", 2), ("gx", 4)
    return pair, [[x, y, z_near, z_far], [y, x, z_near, z_far], [z_near, z_far, x, y]]


def sum_devices(plan, terms, scale):
    width = terms.shape[-1]
    if plan is None or width != 2 * LANES:
        return lax.psum(terms, ("gx", "gy")) * jnp.float32(scale)
    pair, orders = plan
    flat = terms.reshape(-1, width)
    part_rows = flat.shape[0] // PARTS
    stages = len(orders[0]) + 1
    steps = 2 * stages
    out = pl.pallas_call(
        functools.partial(reduce_kernel, pair, orders, scale),
        in_specs=[pl.BlockSpec(memory_space=VMEM)],
        out_specs=pl.BlockSpec(memory_space=VMEM),
        out_shape=jax.ShapeDtypeStruct(flat.shape, jnp.float32),
        scratch_shapes=[VMEM((PARTS, part_rows, LANES), jnp.float32)]
        + [VMEM((PARTS, part_rows >> s, LANES), jnp.float32) for s in range(stages)]
        + [pltpu.SemaphoreType.DMA((steps, PARTS)), pltpu.SemaphoreType.DMA((steps, PARTS))],
        compiler_params=pltpu.CompilerParams(
            collective_id=0, has_side_effects=True, vmem_limit_bytes=48 * 2**20
        ),
    )(flat)
    return out.reshape(terms.shape)


def shards(plan, features, cotangent, kernel, occupancy, neighbors):
    slots = features.shape[0]
    width = features.shape[-1]
    mask_b = occupancy.reshape(slots, 8, 8, 8, 1).astype(jnp.bfloat16)
    mask_f = occupancy.reshape(slots * 512, 1).astype(jnp.float32)
    masked = features * mask_b
    masked_grad = cotangent * mask_b
    both = jnp.stack([masked, masked_grad])
    shifted = z_shifted(both, neighbors)
    even = shifted.reshape(3, 2, slots, 10, 80, width)
    odd = shifted[:, :, :, :, 1:9].reshape(3, 2, slots, 10, 64, width)
    flipped = jnp.flip(kernel, 0).transpose(0, 2, 1)
    grad_t = masked_grad.reshape(-1, width).T
    out, back, terms = conv(even, odd, kernel, flipped, grad_t, mask_f)
    scale = 1.0 / (512.0 * slots * lax.axis_size("gx") * lax.axis_size("gy")) ** 0.5
    kernel_grad = sum_devices(plan, terms, scale)
    return out.reshape(features.shape), back.reshape(features.shape), kernel_grad


def solution(mesh):
    placed = (
        P(("gx", "gy"), None, None, None, None),
        P(("gx", "gy"), None, None, None, None),
        P(),
        P(("gx", "gy"), None),
        P(("gx", "gy"), None),
    )
    plan = sum_plan(mesh, 27 * 256)
    return jax.shard_map(
        functools.partial(shards, plan),
        mesh=mesh,
        in_specs=placed,
        out_specs=(
            P(("gx", "gy"), None, None, None, None),
            P(("gx", "gy"), None, None, None, None),
            P(),
        ),
        check_vma=False,
    )
```

```python
import functools

import jax
import jax.numpy as jnp
from jax import lax
from jax.experimental import pallas as pl
from jax.experimental.pallas import tpu as pltpu
from jax.sharding import PartitionSpec as P

MESH = pl.DeviceIdType.MESH
VMEM = pltpu.VMEM
PARTS = 3
LANES = 128
UNITS_AFTER = (2, 1, 1, 0)
UNITS_BACK = (0, 1, 1, 0)


def shift_by_one(cells, axis):
    count = lax.axis_size(axis)
    ends = count - 1
    head = lambda dim: lax.slice_in_dim(cells, 0, 1, axis=dim)
    tail = lambda dim: lax.slice_in_dim(cells, cells.shape[dim] - 1, cells.shape[dim], axis=dim)
    up = [(i, i + 1) for i in range(ends)]
    down = [(i + 1, i) for i in range(ends)]
    return lambda dim: jnp.concatenate(
        [lax.ppermute(tail(dim), axis, up), cells, lax.ppermute(head(dim), axis, down)], axis=dim
    )


def spread(table, dim):
    first = lax.slice_in_dim(table, 0, 1, axis=dim)
    middle = lax.slice_in_dim(table, 1, 2, axis=dim)
    last = lax.slice_in_dim(table, 2, 3, axis=dim)
    return jnp.concatenate([first] + [middle] * 8 + [last], axis=dim)


def z_shifted(both, neighbors):
    slots = both.shape[1]
    wide = shift_by_one(both, "gx")(2)
    wide = shift_by_one(wide, "gy")(3)
    table = spread(spread(neighbors.reshape(slots, 3, 3, 3), 1), 2)

    def pick(layer, oz):
        total = None
        for slot in range(slots):
            hit = (table[:, :, :, oz] == slot)[None, :, :, :, None, None]
            part = jnp.where(hit, wide[:, slot : slot + 1, :, :, layer], jnp.zeros((), wide.dtype))
            total = part if total is None else total + part
        return total

    low = pick(slice(7, 8), 0)
    mid = pick(slice(0, 8), 1)
    high = pick(slice(0, 1), 2)
    return jnp.stack(
        [
            jnp.concatenate([low, mid[..., :7, :]], 4),
            mid,
            jnp.concatenate([mid[..., 1:, :], high], 4),
        ]
    )


def encode(values):
    peak = jnp.maximum(jnp.max(jnp.abs(values), axis=0, keepdims=True), 1e-33)
    return jnp.round(values * (32767.0 / peak)).astype(jnp.int32).astype(jnp.int16), peak * (1.0 / 32767.0)


def decode(code, unit):
    return code.astype(jnp.int32).astype(jnp.float32) * unit


def conv_kernel(plan, slots, scale, even_ref, odd_ref, w_ref, grad_t_ref, out_ref, back_ref, *rest):
    width = w_ref.shape[-1]

    def window(tensor, brick, ox, oy, oz):
        if oy == 1:
            value = odd_ref[oz, tensor, brick, ox : ox + 8]
        else:
            value = even_ref[oz, tensor, brick, ox : ox + 8, 8 * oy : 8 * oy + 64]
        return value.reshape(512, width)

    def grad_terms(ox, terms_ref):
        for oy in range(3):
            for oz in range(3):
                both = jnp.concatenate([window(0, brick, ox, oy, oz) for brick in range(slots)], 0)
                term = jnp.dot(grad_t_ref[...], both, preferred_element_type=jnp.float32)
                offset = 9 * ox + 3 * oy + oz
                terms_ref[offset * width : (offset + 1) * width] = term.T

    def features_unit(tensor, ox, acc):
        for oy in range(3):
            first = 9 * ox + 3 * oy
            if tensor == 0:
                rhs = w_ref[first : first + 3].reshape(3 * width, width)
            else:
                rhs = jnp.concatenate([w_ref[26 - first - oz] for oz in range(3)], 1)
            for brick in range(slots):
                rows = slice(512 * brick, 512 * brick + 512)
                lhs = jnp.concatenate([window(tensor, brick, ox, oy, oz) for oz in range(3)], 1)
                part = lax.dot_general(
                    lhs, rhs, (((1,), (tensor,)), ((), ())), preferred_element_type=jnp.float32
                )
                if ox == 0 and oy == 0:
                    acc[rows] = part
                else:
                    acc[rows] += part

    def units(accs):
        for tensor, acc, target in ((0, accs[0], out_ref), (1, accs[1], back_ref)):
            for ox in range(3):
                features_unit(tensor, ox, acc)
                if ox == 2:
                    target[...] = acc[...].astype(target.dtype)
                yield

    if plan is None:
        terms_ref, *accs = rest
        for ox in range(3):
            grad_terms(ox, terms_ref)
        for _ in units(accs):
            pass
        return

    pair, orders = plan
    stages = len(orders[0]) + 1
    code_out, unit_out, terms_ref, acc, *accs = rest[:6]
    buffers = rest[6 : 6 + 4 * stages]
    code_to, code_in, unit_to, unit_in = (buffers[i * stages : (i + 1) * stages] for i in range(4))
    send_sem, recv_sem = rest[6 + 4 * stages :]
    part_rows = acc.shape[1]
    block = part_rows >> (stages - 1)
    part_blocks = part_rows // block
    place = {"gx": lax.axis_index("gx"), "gy": lax.axis_index("gy")}

    def bit_of(bit):
        axis, step = bit
        return (place[axis] // step) % 2

    def partner(bit):
        axis, step = bit
        there = dict(place)
        there[axis] = place[axis] + step - 2 * step * bit_of(bit)
        return (there["gx"], there["gy"])

    barrier = pltpu.get_barrier_semaphore()
    for bit in [pair] + sorted(orders[0]):
        pl.semaphore_signal(barrier, inc=1, device_id=partner(bit), device_id_type=MESH)

    side = bit_of(pair)
    mine = pl.ds(pl.multiple_of(side * LANES, LANES), LANES)
    other = pl.ds(pl.multiple_of((1 - side) * LANES, LANES), LANES)
    started = []
    flying = [None] * PARTS

    def send(spans, step, part, bit):
        flying[part] = []
        for which, (src, dst) in enumerate(spans):
            copy = pltpu.make_async_remote_copy(
                src_ref=src,
                dst_ref=dst,
                send_sem=send_sem.at[step, part, which],
                recv_sem=recv_sem.at[step, part, which],
                device_id=partner(bit),
                device_id_type=MESH,
            )
            copy.start()
            started.append(copy)
            flying[part].append(copy)

    def arrived(part):
        for copy in flying[part]:
            copy.wait_recv()

    def rows_at(first):
        return pl.ds(pl.multiple_of(first, 16), block)

    def send_coded(stage, part, bit):
        send(
            [
                (code_to[stage].at[part], code_in[stage].at[part]),
                (unit_to[stage].at[part], unit_in[stage].at[part]),
            ],
            stage,
            part,
            bit,
        )

    work = units(accs)
    base = [0] * PARTS
    for p in range(PARTS):
        grad_terms(p, terms_ref)

        @pl.loop(0, part_blocks)
        def _(i):
            code, unit = encode(terms_ref[rows_at(p * part_rows + i * block), other])
            code_to[0][p, rows_at(i * block)] = code
            unit_to[0][p, i] = unit

        if p == 0:
            pl.semaphore_wait(barrier, stages)
        send_coded(0, p, pair)

    for stage in range(stages):
        blocks = part_blocks >> stage
        for p in range(PARTS):
            arrived(p)

            @pl.loop(0, blocks)
            def _(i):
                value = decode(code_in[stage][p, rows_at(i * block)], unit_in[stage][p, i])
                if stage == 0:
                    own = terms_ref[rows_at(p * part_rows + i * block), mine]
                else:
                    own = acc[p, rows_at((base[p] + i) * block)]
                acc[p, rows_at((base[p] + i) * block)] = own + value

            if stage < stages - 1:
                bit = orders[p][stage]
                half = blocks // 2
                away = base[p] + (1 - bit_of(bit)) * half
                base[p] = base[p] + bit_of(bit) * half

                @pl.loop(0, half)
                def _(i):
                    code, unit = encode(acc[p, rows_at((away + i) * block)])
                    code_to[stage + 1][p, rows_at(i * block)] = code
                    unit_to[stage + 1][p, i] = unit

                send_coded(stage + 1, p, bit)
            else:
                code, unit = encode(acc[p, rows_at(base[p] * block)] * scale)
                code_out[rows_at(p * part_rows + base[p] * block), mine] = code
                unit_out[side, p * part_blocks + base[p]] = unit
        for _ in range(UNITS_AFTER[stage] if stage < stages - 1 else 0):
            next(work, None)
        if stage < stages - 1:
            continue
        for p in range(PARTS):
            code_span = code_out.at[rows_at(p * part_rows + base[p] * block), mine]
            unit_span = unit_out.at[side, pl.ds(p * part_blocks + base[p], 1)]
            send([(code_span, code_span), (unit_span, unit_span)], stages, p, orders[p][-1])

    for back in range(1, stages + 1):
        level = stages - 1 - back
        for p in range(PARTS):
            arrived(p)
            if level < 0:
                continue
            blocks = part_blocks >> level
            base[p] = base[p] - bit_of(orders[p][level]) * (blocks // 2)
            first = pl.multiple_of(p * part_rows + base[p] * block, 16)
            code_span = code_out.at[pl.ds(first, blocks * block), mine]
            unit_span = unit_out.at[side, pl.ds(p * part_blocks + base[p], blocks)]
            bit = orders[p][level - 1] if level > 0 else pair
            send([(code_span, code_span), (unit_span, unit_span)], stages + back, p, bit)
        if level >= 0:
            for _ in range(UNITS_BACK[back - 1]):
                next(work, None)
    for _ in work:
        pass
    for copy in started:
        copy.wait_send()


def sum_plan(mesh, rows):
    sizes = dict(mesh.shape)
    if sizes["gx"] != 8 or sizes["gy"] != 4 or rows % (PARTS * 16 * 16):
        return None
    pair, x, y, z_near, z_far = ("gy", 1), ("gy", 2), ("gx", 1), ("gx", 2), ("gx", 4)
    return pair, [[x, y, z_near, z_far], [y, x, z_near, z_far], [z_near, z_far, x, y]]


def conv(plan, even, odd, weights, grad_t, scale):
    slots = even.shape[2]
    width = even.shape[-1]
    rows = slots * 512
    offsets = weights.shape[0]
    vmem = pl.BlockSpec(memory_space=VMEM)
    outs = [jax.ShapeDtypeStruct((rows, width), jnp.bfloat16)] * 2
    accs = [VMEM((rows, width), jnp.float32)] * 2
    full = (offsets * width, width)
    if plan is None:
        outs = outs + [jax.ShapeDtypeStruct(full, jnp.float32)]
        scratch = accs
        params = pltpu.CompilerParams(vmem_limit_bytes=58 * 2**20)
    else:
        stages = len(plan[1][0]) + 1
        part_rows = offsets * width // PARTS
        part_blocks = 1 << (stages - 1)
        outs = outs + [
            jax.ShapeDtypeStruct(full, jnp.int16),
            jax.ShapeDtypeStruct((2, PARTS * part_blocks, 1, LANES), jnp.float32),
        ]
        codes = [VMEM((PARTS, part_rows >> s, LANES), jnp.int16) for s in range(stages)]
        units = [VMEM((PARTS, part_blocks >> s, 1, LANES), jnp.float32) for s in range(stages)]
        sems = pltpu.SemaphoreType.DMA((2 * stages, PARTS, 2))
        scratch = (
            [VMEM(full, jnp.float32), VMEM((PARTS, part_rows, LANES), jnp.float32)]
            + accs
            + codes
            + codes
            + units
            + units
            + [sems, sems]
        )
        params = pltpu.CompilerParams(
            collective_id=0, has_side_effects=True, vmem_limit_bytes=58 * 2**20
        )
    return pl.pallas_call(
        functools.partial(conv_kernel, plan, slots, scale),
        in_specs=[vmem] * 4,
        out_specs=[vmem] * len(outs),
        out_shape=outs,
        scratch_shapes=scratch,
        compiler_params=params,
        cost_estimate=pl.CostEstimate(
            flops=offsets * 6 * rows * width * width, bytes_accessed=24 * 2**20, transcendentals=0
        ),
    )(even, odd, weights, grad_t)


def shards(plan, features, cotangent, kernel, occupancy, neighbors):
    slots = features.shape[0]
    width = features.shape[-1]
    mask_b = occupancy.reshape(slots, 8, 8, 8, 1).astype(jnp.bfloat16)
    masked = features * mask_b
    masked_grad = cotangent * mask_b
    both = jnp.stack([masked, masked_grad])
    shifted = z_shifted(both, neighbors)
    even = shifted.reshape(3, 2, slots, 10, 80, width)
    odd = shifted[:, :, :, :, 1:9].reshape(3, 2, slots, 10, 64, width)
    grad_t = masked_grad.reshape(-1, width).T
    scale = 1.0 / (512.0 * slots * lax.axis_size("gx") * lax.axis_size("gy")) ** 0.5
    if width != 2 * LANES:
        plan = None
    out, back, *total = conv(plan, even, odd, kernel, grad_t, scale)
    if plan is None:
        kernel_grad = lax.psum(total[0], ("gx", "gy")) * jnp.float32(scale)
    else:
        code, unit = total
        blocks = unit.shape[1]
        unit = unit.transpose(1, 2, 0, 3).reshape(blocks, 1, width)
        kernel_grad = decode(code.reshape(blocks, -1, width), unit)
    return (
        out.reshape(features.shape) * mask_b,
        back.reshape(features.shape) * mask_b,
        kernel_grad.reshape(kernel.shape),
    )


def solution(mesh):
    placed = (
        P(("gx", "gy"), None, None, None, None),
        P(("gx", "gy"), None, None, None, None),
        P(),
        P(("gx", "gy"), None),
        P(("gx", "gy"), None),
    )
    plan = sum_plan(mesh, 27 * 256)
    return jax.shard_map(
        functools.partial(shards, plan),
        mesh=mesh,
        in_specs=placed,
        out_specs=(
            P(("gx", "gy"), None, None, None, None),
            P(("gx", "gy"), None, None, None, None),
            P(),
        ),
        check_vma=False,
    )
```

```python
import functools

import jax
import jax.numpy as jnp
from jax import lax
from jax.experimental import pallas as pl
from jax.experimental.pallas import tpu as pltpu
from jax.sharding import PartitionSpec as P

MESH = pl.DeviceIdType.MESH
VMEM = pltpu.VMEM
PARTS = 3
LANES = 128
HALO = ((-1, 0), (1, 0), (0, -1), (0, 1), (-1, -1), (-1, 1), (1, -1), (1, 1))
UNITS_AFTER = (2, 1, 1, 0)
UNITS_BACK = (0, 1, 1, 0)


def shift_by_one(cells, axis):
    count = lax.axis_size(axis)
    ends = count - 1
    head = lambda dim: lax.slice_in_dim(cells, 0, 1, axis=dim)
    tail = lambda dim: lax.slice_in_dim(cells, cells.shape[dim] - 1, cells.shape[dim], axis=dim)
    up = [(i, i + 1) for i in range(ends)]
    down = [(i + 1, i) for i in range(ends)]
    return lambda dim: jnp.concatenate(
        [lax.ppermute(tail(dim), axis, up), cells, lax.ppermute(head(dim), axis, down)], axis=dim
    )


def spread(table, dim):
    first = lax.slice_in_dim(table, 0, 1, axis=dim)
    middle = lax.slice_in_dim(table, 1, 2, axis=dim)
    last = lax.slice_in_dim(table, 2, 3, axis=dim)
    return jnp.concatenate([first] + [middle] * 8 + [last], axis=dim)


def z_shifted(both, neighbors):
    slots = both.shape[1]
    wide = shift_by_one(both, "gx")(2)
    wide = shift_by_one(wide, "gy")(3)
    table = spread(spread(neighbors.reshape(slots, 3, 3, 3), 1), 2)

    def pick(layer, oz):
        total = None
        for slot in range(slots):
            hit = (table[:, :, :, oz] == slot)[None, :, :, :, None, None]
            part = jnp.where(hit, wide[:, slot : slot + 1, :, :, layer], jnp.zeros((), wide.dtype))
            total = part if total is None else total + part
        return total

    low = pick(slice(7, 8), 0)
    mid = pick(slice(0, 8), 1)
    high = pick(slice(0, 1), 2)
    return jnp.stack(
        [
            jnp.concatenate([low, mid[..., :7, :]], 4),
            mid,
            jnp.concatenate([mid[..., 1:, :], high], 4),
        ]
    )


def encode(values):
    peak = jnp.maximum(jnp.max(jnp.abs(values), axis=0, keepdims=True), 1e-33)
    return jnp.round(values * (32767.0 / peak)).astype(jnp.int32).astype(jnp.int16), peak * (1.0 / 32767.0)


def decode(code, unit):
    return code.astype(jnp.int32).astype(jnp.float32) * unit


def conv_kernel(plan, slots, scale, *refs):
    if plan is None:
        even_ref, odd_ref, w_ref, grad_t_ref, out_ref, back_ref, *rest = refs
    else:
        both_ref, y_ref, corner_ref, near_ref, w_ref, grad_t_ref, out_ref, back_ref, *rest = refs
    width = w_ref.shape[-1]

    def window(tensor, brick, ox, oy, oz):
        if oy == 1:
            value = odd_ref[oz, tensor, brick, ox : ox + 8]
        else:
            value = even_ref[oz, tensor, brick, ox : ox + 8, 8 * oy : 8 * oy + 64]
        return value.reshape(512, width)

    def grad_terms(ox, terms_ref):
        for oy in range(3):
            for oz in range(3):
                both = jnp.concatenate([window(0, brick, ox, oy, oz) for brick in range(slots)], 0)
                term = jnp.dot(grad_t_ref[...], both, preferred_element_type=jnp.float32)
                offset = 9 * ox + 3 * oy + oz
                terms_ref[offset * width : (offset + 1) * width] = term.T

    def features_unit(tensor, ox, acc):
        for oy in range(3):
            first = 9 * ox + 3 * oy
            if tensor == 0:
                rhs = w_ref[first : first + 3].reshape(3 * width, width)
            else:
                rhs = jnp.concatenate([w_ref[26 - first - oz] for oz in range(3)], 1)
            for brick in range(slots):
                rows = slice(512 * brick, 512 * brick + 512)
                lhs = jnp.concatenate([window(tensor, brick, ox, oy, oz) for oz in range(3)], 1)
                part = lax.dot_general(
                    lhs, rhs, (((1,), (tensor,)), ((), ())), preferred_element_type=jnp.float32
                )
                if ox == 0 and oy == 0:
                    acc[rows] = part
                else:
                    acc[rows] += part

    def units(accs):
        for tensor, acc, target in ((0, accs[0], out_ref), (1, accs[1], back_ref)):
            for ox in range(3):
                features_unit(tensor, ox, acc)
                if ox == 2:
                    target[...] = acc[...].astype(target.dtype)
                yield

    if plan is None:
        terms_ref, *accs = rest
        for ox in range(3):
            grad_terms(ox, terms_ref)
        for _ in units(accs):
            pass
        return

    pair, orders = plan
    stages = len(orders[0]) + 1
    code_out, unit_out, terms_ref, acc, *accs = rest[:6]
    buffers = rest[6 : 6 + 4 * stages]
    code_to, code_in, unit_to, unit_in = (buffers[i * stages : (i + 1) * stages] for i in range(4))
    send_sem, recv_sem, even_ref, odd_ref, *halo = rest[6 + 4 * stages :]
    halo_x, halo_y, halo_corner, edge_y, halo_send, halo_recv = halo
    part_rows = acc.shape[1]
    block = part_rows >> (stages - 1)
    part_blocks = part_rows // block
    place = {"gx": lax.axis_index("gx"), "gy": lax.axis_index("gy")}

    def bit_of(bit):
        axis, step = bit
        return (place[axis] // step) % 2

    def partner(bit):
        axis, step = bit
        there = dict(place)
        there[axis] = place[axis] + step - 2 * step * bit_of(bit)
        return (there["gx"], there["gy"])

    barrier = pltpu.get_barrier_semaphore()
    for bit in [pair] + sorted(orders[0]):
        pl.semaphore_signal(barrier, inc=1, device_id=partner(bit), device_id_type=MESH)

    def inside(sign, step):
        col_x, col_y = place["gx"] + sign * step[0], place["gy"] + sign * step[1]
        x_in = (col_x >= 0) & (col_x < lax.axis_size("gx"))
        return x_in & (col_y >= 0) & (col_y < lax.axis_size("gy"))

    def halo_copy(slot, sign):
        step = HALO[slot]
        low_x, low_y = int(step[0] > 0), int(step[1] > 0)
        if step[1] == 0:
            src, dst = both_ref.at[:, :, 0 if low_x else 7], halo_x.at[low_x]
        elif step[0] == 0:
            src, dst = y_ref.at[1 - low_y], halo_y.at[low_y]
        else:
            src, dst = corner_ref.at[1 - low_x, 1 - low_y], halo_corner.at[low_x, low_y]
        there = (place["gx"] + sign * step[0], place["gy"] + sign * step[1])
        return dst, pltpu.make_async_remote_copy(
            src_ref=src,
            dst_ref=dst,
            send_sem=halo_send.at[slot],
            recv_sem=halo_recv.at[slot],
            device_id=there,
            device_id_type=MESH,
        )

    near = stages
    for slot, step in enumerate(HALO):
        near = near + inside(1, step).astype(jnp.int32)

        @pl.when(inside(-1, step))
        def _():
            there = (place["gx"] - step[0], place["gy"] - step[1])
            pl.semaphore_signal(barrier, inc=1, device_id=there, device_id_type=MESH)

    pl.semaphore_wait(barrier, near)
    for slot, step in enumerate(HALO):
        @pl.when(inside(-1, step))
        def _():
            halo_copy(slot, -1)[1].start()

    height = lax.broadcasted_iota(jnp.int32, (1, 8, width), 1)

    def extended_z(sources, brick, first):
        def pick(offset):
            slot_row = near_ref[brick * 27 + first + offset]
            total = jnp.zeros_like(sources[0])
            for slot in range(slots):
                total = jnp.where(slot_row[None] == slot, sources[slot], total)
            return total

        low, mid, high = pick(0), pick(1), pick(2)
        return [
            pltpu.roll(jnp.where(height == 7, low, mid), 1, 1),
            mid,
            pltpu.roll(jnp.where(height == 0, high, mid), 7, 1),
        ]

    def cells(value):
        return value.astype(jnp.float32).reshape(-1, 8, width)

    def rows_of(value):
        return value.reshape(-1, width).astype(jnp.bfloat16)

    @pl.loop(0, 2 * slots)
    def _(i):
        tensor, brick = i // slots, i % slots

        @pl.loop(0, 8)
        def _(x):
            sources = [cells(both_ref[tensor, slot, x]) for slot in range(slots)]
            for oz, value in enumerate(extended_z(sources, brick, 12)):
                odd_ref[oz, tensor, brick, x + 1] = rows_of(value)

    for slot, step in enumerate(HALO):
        dst, arriving = halo_copy(slot, 1)

        @pl.when(inside(1, step))
        def _():
            arriving.wait_recv()

        @pl.when(jnp.logical_not(inside(1, step)))
        def _():
            dst[...] = jnp.zeros(dst.shape, dst.dtype)

    @pl.loop(0, 2 * slots)
    def _(i):
        tensor, brick = i // slots, i % slots
        for end in range(2):
            sources = [cells(halo_y[end, tensor, slot]) for slot in range(slots)]
            for oz, value in enumerate(extended_z(sources, brick, 9 + 6 * end)):
                edge_y[oz, end] = value

        @pl.loop(0, 8)
        def _(x):
            for oz in range(3):
                middle = cells(odd_ref[oz, tensor, brick, x + 1])
                row = jnp.concatenate([edge_y[oz, 0, pl.ds(x, 1)], middle, edge_y[oz, 1, pl.ds(x, 1)]], 0)
                even_ref[oz, tensor, brick, x + 1] = rows_of(row)

        for end in range(2):
            first = 18 * end
            middle = extended_z(
                [cells(halo_x[end, tensor, slot]) for slot in range(slots)], brick, first + 3
            )
            ends = []
            for end_y in range(2):
                column = [
                    halo_corner[end, end_y, tensor, slot].astype(jnp.float32)[None, :8]
                    for slot in range(slots)
                ]
                ends.append(extended_z(column, brick, first + 6 * end_y))
            for oz in range(3):
                row = jnp.concatenate([ends[0][oz], middle[oz], ends[1][oz]], 0)
                even_ref[oz, tensor, brick, 9 * end] = rows_of(row)
                odd_ref[oz, tensor, brick, 9 * end] = rows_of(middle[oz])

    side = bit_of(pair)
    mine = pl.ds(pl.multiple_of(side * LANES, LANES), LANES)
    other = pl.ds(pl.multiple_of((1 - side) * LANES, LANES), LANES)
    started = []
    flying = [None] * PARTS

    def send(spans, step, part, bit):
        flying[part] = []
        for which, (src, dst) in enumerate(spans):
            copy = pltpu.make_async_remote_copy(
                src_ref=src,
                dst_ref=dst,
                send_sem=send_sem.at[step, part, which],
                recv_sem=recv_sem.at[step, part, which],
                device_id=partner(bit),
                device_id_type=MESH,
            )
            copy.start()
            started.append(copy)
            flying[part].append(copy)

    def arrived(part):
        for copy in flying[part]:
            copy.wait_recv()

    def rows_at(first):
        return pl.ds(pl.multiple_of(first, 16), block)

    def send_coded(stage, part, bit):
        send(
            [
                (code_to[stage].at[part], code_in[stage].at[part]),
                (unit_to[stage].at[part], unit_in[stage].at[part]),
            ],
            stage,
            part,
            bit,
        )

    work = units(accs)
    base = [0] * PARTS
    for p in range(PARTS):
        grad_terms(p, terms_ref)

        @pl.loop(0, part_blocks)
        def _(i):
            code, unit = encode(terms_ref[rows_at(p * part_rows + i * block), other])
            code_to[0][p, rows_at(i * block)] = code
            unit_to[0][p, i] = unit

        send_coded(0, p, pair)

    for stage in range(stages):
        blocks = part_blocks >> stage
        for p in range(PARTS):
            arrived(p)

            @pl.loop(0, blocks)
            def _(i):
                value = decode(code_in[stage][p, rows_at(i * block)], unit_in[stage][p, i])
                if stage == 0:
                    own = terms_ref[rows_at(p * part_rows + i * block), mine]
                else:
                    own = acc[p, rows_at((base[p] + i) * block)]
                acc[p, rows_at((base[p] + i) * block)] = own + value

            if stage < stages - 1:
                bit = orders[p][stage]
                half = blocks // 2
                away = base[p] + (1 - bit_of(bit)) * half
                base[p] = base[p] + bit_of(bit) * half

                @pl.loop(0, half)
                def _(i):
                    code, unit = encode(acc[p, rows_at((away + i) * block)])
                    code_to[stage + 1][p, rows_at(i * block)] = code
                    unit_to[stage + 1][p, i] = unit

                send_coded(stage + 1, p, bit)
            else:
                code, unit = encode(acc[p, rows_at(base[p] * block)] * scale)
                code_out[rows_at(p * part_rows + base[p] * block), mine] = code
                unit_out[side, p * part_blocks + base[p]] = unit
        for _ in range(UNITS_AFTER[stage] if stage < stages - 1 else 0):
            next(work, None)
        if stage < stages - 1:
            continue
        for p in range(PARTS):
            code_span = code_out.at[rows_at(p * part_rows + base[p] * block), mine]
            unit_span = unit_out.at[side, pl.ds(p * part_blocks + base[p], 1)]
            send([(code_span, code_span), (unit_span, unit_span)], stages, p, orders[p][-1])

    for back in range(1, stages + 1):
        level = stages - 1 - back
        for p in range(PARTS):
            arrived(p)
            if level < 0:
                continue
            blocks = part_blocks >> level
            base[p] = base[p] - bit_of(orders[p][level]) * (blocks // 2)
            first = pl.multiple_of(p * part_rows + base[p] * block, 16)
            code_span = code_out.at[pl.ds(first, blocks * block), mine]
            unit_span = unit_out.at[side, pl.ds(p * part_blocks + base[p], blocks)]
            bit = orders[p][level - 1] if level > 0 else pair
            send([(code_span, code_span), (unit_span, unit_span)], stages + back, p, bit)
        if level >= 0:
            for _ in range(UNITS_BACK[back - 1]):
                next(work, None)
    for _ in work:
        pass
    for copy in started:
        copy.wait_send()
    for slot, step in enumerate(HALO):
        @pl.when(inside(-1, step))
        def _():
            halo_copy(slot, -1)[1].wait_send()


def sum_plan(mesh, rows):
    sizes = dict(mesh.shape)
    if sizes["gx"] != 8 or sizes["gy"] != 4 or rows % (PARTS * 16 * 16):
        return None
    pair, x, y, z_near, z_far = ("gy", 1), ("gy", 2), ("gx", 1), ("gx", 2), ("gx", 4)
    return pair, [[x, y, z_near, z_far], [y, x, z_near, z_far], [z_near, z_far, x, y]]


def conv(plan, slots, scale, *operands):
    weights = operands[-2]
    width = weights.shape[-1]
    rows = slots * 512
    offsets = weights.shape[0]
    vmem = pl.BlockSpec(memory_space=VMEM)
    outs = [jax.ShapeDtypeStruct((rows, width), jnp.bfloat16)] * 2
    accs = [VMEM((rows, width), jnp.float32)] * 2
    full = (offsets * width, width)
    if plan is None:
        outs = outs + [jax.ShapeDtypeStruct(full, jnp.float32)]
        scratch = accs
        params = pltpu.CompilerParams(vmem_limit_bytes=58 * 2**20)
    else:
        stages = len(plan[1][0]) + 1
        part_rows = offsets * width // PARTS
        part_blocks = 1 << (stages - 1)
        outs = outs + [
            jax.ShapeDtypeStruct(full, jnp.int16),
            jax.ShapeDtypeStruct((2, PARTS * part_blocks, 1, LANES), jnp.float32),
        ]
        codes = [VMEM((PARTS, part_rows >> s, LANES), jnp.int16) for s in range(stages)]
        units = [VMEM((PARTS, part_blocks >> s, 1, LANES), jnp.float32) for s in range(stages)]
        sems = pltpu.SemaphoreType.DMA((2 * stages, PARTS, 2))
        scratch = (
            [VMEM(full, jnp.float32), VMEM((PARTS, part_rows, LANES), jnp.float32)]
            + accs
            + codes
            + codes
            + units
            + units
            + [sems, sems]
            + [VMEM((3, 2, slots, 10, wide, width), jnp.bfloat16) for wide in (80, 64)]
            + [VMEM((2, 2, slots, 64, width), jnp.bfloat16)] * 2
            + [VMEM((2, 2, 2, slots, 16, width), jnp.bfloat16)]
            + [VMEM((3, 2, 8, 8, width), jnp.float32)]
            + [pltpu.SemaphoreType.DMA((8,))] * 2
        )
        params = pltpu.CompilerParams(
            collective_id=0, has_side_effects=True, vmem_limit_bytes=58 * 2**20
        )
    return pl.pallas_call(
        functools.partial(conv_kernel, plan, slots, scale),
        in_specs=[vmem] * len(operands),
        out_specs=[vmem] * len(outs),
        out_shape=outs,
        scratch_shapes=scratch,
        compiler_params=params,
        cost_estimate=pl.CostEstimate(
            flops=offsets * 6 * rows * width * width, bytes_accessed=24 * 2**20, transcendentals=0
        ),
    )(*operands)


def decode_kernel(code_ref, unit_ref, out_ref):
    steps = unit_ref.shape[1]
    block = code_ref.shape[0] // steps
    for i in range(steps):
        for side in range(2):
            at = slice(i * block, (i + 1) * block), slice(side * LANES, (side + 1) * LANES)
            out_ref[at] = decode(code_ref[at], unit_ref[side, i])


def decode_all(code, unit):
    rows, width = code.shape
    steps = 8
    tile = pl.BlockSpec((rows // steps, width), lambda i: (i, 0))
    return pl.pallas_call(
        decode_kernel,
        grid=(steps,),
        in_specs=[tile, pl.BlockSpec((2, unit.shape[1] // steps, 1, LANES), lambda i: (0, i, 0, 0))],
        out_specs=tile,
        out_shape=jax.ShapeDtypeStruct(code.shape, jnp.float32),
        compiler_params=pltpu.CompilerParams(vmem_limit_bytes=24 * 2**20),
        cost_estimate=pl.CostEstimate(flops=2 * rows * width, bytes_accessed=6 * rows * width, transcendentals=0),
    )(code, unit)


def shards(plan, features, cotangent, kernel, occupancy, neighbors):
    slots = features.shape[0]
    width = features.shape[-1]
    mask_b = occupancy.reshape(slots, 8, 8, 8, 1).astype(jnp.bfloat16)
    masked = features * mask_b
    masked_grad = cotangent * mask_b
    both = jnp.stack([masked, masked_grad])
    grad_t = masked_grad.reshape(-1, width).T
    scale = 1.0 / (512.0 * slots * lax.axis_size("gx") * lax.axis_size("gy")) ** 0.5
    if width != 2 * LANES:
        plan = None
    if plan is None:
        shifted = z_shifted(both, neighbors)
        even = shifted.reshape(3, 2, slots, 10, 80, width)
        odd = shifted[:, :, :, :, 1:9].reshape(3, 2, slots, 10, 64, width)
        operands = even, odd
    else:
        sides = jnp.stack([both[:, :, :, 0], both[:, :, :, 7]])
        corners = jnp.stack([sides[:, :, :, 0], sides[:, :, :, 7]])
        corners = jnp.concatenate([corners, jnp.zeros_like(corners)], -2)
        near = jnp.broadcast_to(neighbors.reshape(-1, 1, 1), (neighbors.size, 1, width))
        operands = both.reshape(2, slots, 8, 64, width), sides.reshape(2, 2, slots, 64, width), corners, near
    out, back, *total = conv(plan, slots, scale, *operands, kernel, grad_t)
    if plan is None:
        kernel_grad = lax.psum(total[0], ("gx", "gy")) * jnp.float32(scale)
    else:
        kernel_grad = decode_all(*total)
    return (
        out.reshape(features.shape) * mask_b,
        back.reshape(features.shape) * mask_b,
        kernel_grad.reshape(kernel.shape),
    )


def solution(mesh):
    placed = (
        P(("gx", "gy"), None, None, None, None),
        P(("gx", "gy"), None, None, None, None),
        P(),
        P(("gx", "gy"), None),
        P(("gx", "gy"), None),
    )
    plan = sum_plan(mesh, 27 * 256)
    return jax.shard_map(
        functools.partial(shards, plan),
        mesh=mesh,
        in_specs=placed,
        out_specs=(
            P(("gx", "gy"), None, None, None, None),
            P(("gx", "gy"), None, None, None, None),
            P(),
        ),
        check_vma=False,
    )
```

```python
import functools

import jax
import jax.numpy as jnp
from jax import lax
from jax.experimental import pallas as pl
from jax.experimental.pallas import tpu as pltpu
from jax.sharding import PartitionSpec as P

MESH = pl.DeviceIdType.MESH
VMEM = pltpu.VMEM
PARTS = 3
LANES = 128
HALO = ((-1, 0), (1, 0), (0, -1), (0, 1), (-1, -1), (-1, 1), (1, -1), (1, 1))
EVENTS = (0, 1, 0, 1, 2, 0, 2, 1, 0, 2, 1, 0, 0, 2, 1, 1, 2, 0, 2, 1, 2, 0, 1, 2)
DOUBLE = (1, 4)


def shift_by_one(cells, axis):
    count = lax.axis_size(axis)
    ends = count - 1
    head = lambda dim: lax.slice_in_dim(cells, 0, 1, axis=dim)
    tail = lambda dim: lax.slice_in_dim(cells, cells.shape[dim] - 1, cells.shape[dim], axis=dim)
    up = [(i, i + 1) for i in range(ends)]
    down = [(i + 1, i) for i in range(ends)]
    return lambda dim: jnp.concatenate(
        [lax.ppermute(tail(dim), axis, up), cells, lax.ppermute(head(dim), axis, down)], axis=dim
    )


def spread(table, dim):
    first = lax.slice_in_dim(table, 0, 1, axis=dim)
    middle = lax.slice_in_dim(table, 1, 2, axis=dim)
    last = lax.slice_in_dim(table, 2, 3, axis=dim)
    return jnp.concatenate([first] + [middle] * 8 + [last], axis=dim)


def z_shifted(both, neighbors):
    slots = both.shape[1]
    wide = shift_by_one(both, "gx")(2)
    wide = shift_by_one(wide, "gy")(3)
    table = spread(spread(neighbors.reshape(slots, 3, 3, 3), 1), 2)

    def pick(layer, oz):
        total = None
        for slot in range(slots):
            hit = (table[:, :, :, oz] == slot)[None, :, :, :, None, None]
            part = jnp.where(hit, wide[:, slot : slot + 1, :, :, layer], jnp.zeros((), wide.dtype))
            total = part if total is None else total + part
        return total

    low = pick(slice(7, 8), 0)
    mid = pick(slice(0, 8), 1)
    high = pick(slice(0, 1), 2)
    return jnp.stack(
        [
            jnp.concatenate([low, mid[..., :7, :]], 4),
            mid,
            jnp.concatenate([mid[..., 1:, :], high], 4),
        ]
    )


def encode(values):
    peak = jnp.maximum(jnp.max(jnp.abs(values), axis=0, keepdims=True), 1e-33)
    return jnp.round(values * (32767.0 / peak)).astype(jnp.int32).astype(jnp.int16), peak * (1.0 / 32767.0)


def decode(code, unit):
    return code.astype(jnp.int32).astype(jnp.float32) * unit


def conv_kernel(plan, slots, scale, *refs):
    if plan is None:
        even_ref, odd_ref, w_ref, grad_t_ref, out_ref, back_ref, *rest = refs
    else:
        both_ref, y_ref, corner_ref, near_ref, w_ref, grad_t_ref, out_ref, back_ref, *rest = refs
    width = w_ref.shape[-1]

    def window(tensor, brick, ox, oy, oz):
        if oy == 1:
            value = odd_ref[oz, tensor, brick, ox : ox + 8]
        else:
            value = even_ref[oz, tensor, brick, ox : ox + 8, 8 * oy : 8 * oy + 64]
        return value.reshape(512, width)

    def grad_terms(ox, terms_ref):
        for oy in range(3):
            for oz in range(3):
                both = jnp.concatenate([window(0, brick, ox, oy, oz) for brick in range(slots)], 0)
                term = jnp.dot(grad_t_ref[...], both, preferred_element_type=jnp.float32)
                offset = 9 * ox + 3 * oy + oz
                terms_ref[offset * width : (offset + 1) * width] = term.T

    def features_unit(tensor, ox, oy, acc):
        first = 9 * ox + 3 * oy
        if tensor == 0:
            rhs = w_ref[first : first + 3].reshape(3 * width, width)
        else:
            rhs = jnp.concatenate([w_ref[26 - first - oz] for oz in range(3)], 1)
        for brick in range(slots):
            rows = slice(512 * brick, 512 * brick + 512)
            lhs = jnp.concatenate([window(tensor, brick, ox, oy, oz) for oz in range(3)], 1)
            part = lax.dot_general(
                lhs, rhs, (((1,), (tensor,)), ((), ())), preferred_element_type=jnp.float32
            )
            if first == 0:
                acc[rows] = part
            else:
                acc[rows] += part

    def units(accs, prepare):
        for tensor, acc, target in ((0, accs[0], out_ref), (1, accs[1], back_ref)):
            for action in prepare[tensor]:
                action()
                yield
            for ox in range(3):
                for oy in range(3):
                    features_unit(tensor, ox, oy, acc)
                    if ox == 2 and oy == 2:
                        target[...] = acc[...].astype(target.dtype)
                    yield

    if plan is None:
        terms_ref, *accs = rest
        for ox in range(3):
            grad_terms(ox, terms_ref)
        for _ in units(accs, ((), ())):
            pass
        return

    pair, orders = plan
    stages = len(orders[0]) + 1
    code_out, unit_out, terms_ref, acc, *accs = rest[:6]
    buffers = rest[6 : 6 + 4 * stages]
    code_to, code_in, unit_to, unit_in = (buffers[i * stages : (i + 1) * stages] for i in range(4))
    send_sem, recv_sem, even_ref, odd_ref, *halo = rest[6 + 4 * stages :]
    halo_x, halo_y, halo_corner, edge_y, halo_send, halo_recv = halo
    part_rows = acc.shape[1]
    block = part_rows >> (stages - 1)
    part_blocks = part_rows // block
    place = {"gx": lax.axis_index("gx"), "gy": lax.axis_index("gy")}

    def bit_of(bit):
        axis, step = bit
        return (place[axis] // step) % 2

    def partner(bit):
        axis, step = bit
        there = dict(place)
        there[axis] = place[axis] + step - 2 * step * bit_of(bit)
        return (there["gx"], there["gy"])

    barrier = pltpu.get_barrier_semaphore()
    for bit in [pair] + sorted(orders[0]):
        pl.semaphore_signal(barrier, inc=1, device_id=partner(bit), device_id_type=MESH)

    def inside(sign, step):
        col_x, col_y = place["gx"] + sign * step[0], place["gy"] + sign * step[1]
        x_in = (col_x >= 0) & (col_x < lax.axis_size("gx"))
        return x_in & (col_y >= 0) & (col_y < lax.axis_size("gy"))

    def halo_copy(slot, sign):
        step = HALO[slot]
        low_x, low_y = int(step[0] > 0), int(step[1] > 0)
        if step[1] == 0:
            src, dst = both_ref.at[:, :, 0 if low_x else 7], halo_x.at[low_x]
        elif step[0] == 0:
            src, dst = y_ref.at[1 - low_y], halo_y.at[low_y]
        else:
            src, dst = corner_ref.at[1 - low_x, 1 - low_y], halo_corner.at[low_x, low_y]
        there = (place["gx"] + sign * step[0], place["gy"] + sign * step[1])
        return dst, pltpu.make_async_remote_copy(
            src_ref=src,
            dst_ref=dst,
            send_sem=halo_send.at[slot],
            recv_sem=halo_recv.at[slot],
            device_id=there,
            device_id_type=MESH,
        )

    near = stages
    for slot, step in enumerate(HALO):
        near = near + inside(1, step).astype(jnp.int32)

        @pl.when(inside(-1, step))
        def _():
            there = (place["gx"] - step[0], place["gy"] - step[1])
            pl.semaphore_signal(barrier, inc=1, device_id=there, device_id_type=MESH)

    pl.semaphore_wait(barrier, near)
    for slot, step in enumerate(HALO):
        @pl.when(inside(-1, step))
        def _():
            halo_copy(slot, -1)[1].start()

    height = lax.broadcasted_iota(jnp.int32, (1, 8, width), 1)

    def extended_z(sources, brick, first):
        def pick(offset):
            slot_row = near_ref[brick * 27 + first + offset]
            total = jnp.zeros_like(sources[0])
            for slot in range(slots):
                total = jnp.where(slot_row[None] == slot, sources[slot], total)
            return total

        low, mid, high = pick(0), pick(1), pick(2)
        return [
            pltpu.roll(jnp.where(height == 7, low, mid), 1, 1),
            mid,
            pltpu.roll(jnp.where(height == 0, high, mid), 7, 1),
        ]

    def cells(value):
        return value.astype(jnp.float32).reshape(-1, 8, width)

    def rows_of(value):
        return value.reshape(-1, width).astype(jnp.bfloat16)

    def build_center(tensor):
        @pl.loop(0, slots)
        def _(brick):

            @pl.loop(0, 8)
            def _(x):
                sources = [cells(both_ref[tensor, slot, x]) for slot in range(slots)]
                for oz, value in enumerate(extended_z(sources, brick, 12)):
                    odd_ref[oz, tensor, brick, x + 1] = rows_of(value)

    def build_edges(tensor):
        @pl.loop(0, slots)
        def _(brick):
            for end in range(2):
                sources = [cells(halo_y[end, tensor, slot]) for slot in range(slots)]
                for oz, value in enumerate(extended_z(sources, brick, 9 + 6 * end)):
                    edge_y[oz, end] = value

            @pl.loop(0, 8)
            def _(x):
                for oz in range(3):
                    middle = cells(odd_ref[oz, tensor, brick, x + 1])
                    row = jnp.concatenate([edge_y[oz, 0, pl.ds(x, 1)], middle, edge_y[oz, 1, pl.ds(x, 1)]], 0)
                    even_ref[oz, tensor, brick, x + 1] = rows_of(row)

            for end in range(2):
                first = 18 * end
                middle = extended_z(
                    [cells(halo_x[end, tensor, slot]) for slot in range(slots)], brick, first + 3
                )
                ends = []
                for end_y in range(2):
                    column = [
                        halo_corner[end, end_y, tensor, slot].astype(jnp.float32)[None, :8]
                        for slot in range(slots)
                    ]
                    ends.append(extended_z(column, brick, first + 6 * end_y))
                for oz in range(3):
                    row = jnp.concatenate([ends[0][oz], middle[oz], ends[1][oz]], 0)
                    even_ref[oz, tensor, brick, 9 * end] = rows_of(row)
                    odd_ref[oz, tensor, brick, 9 * end] = rows_of(middle[oz])

    build_center(0)
    for slot, step in enumerate(HALO):
        dst, arriving = halo_copy(slot, 1)

        @pl.when(inside(1, step))
        def _():
            arriving.wait_recv()

        @pl.when(jnp.logical_not(inside(1, step)))
        def _():
            dst[...] = jnp.zeros(dst.shape, dst.dtype)

    build_edges(0)
    side = bit_of(pair)
    mine = pl.ds(pl.multiple_of(side * LANES, LANES), LANES)
    other = pl.ds(pl.multiple_of((1 - side) * LANES, LANES), LANES)
    started = []
    flying = [None] * PARTS

    def send(spans, step, part, bit):
        flying[part] = []
        for which, (src, dst) in enumerate(spans):
            copy = pltpu.make_async_remote_copy(
                src_ref=src,
                dst_ref=dst,
                send_sem=send_sem.at[step, part, which],
                recv_sem=recv_sem.at[step, part, which],
                device_id=partner(bit),
                device_id_type=MESH,
            )
            copy.start()
            started.append(copy)
            flying[part].append(copy)

    def arrived(part):
        for copy in flying[part]:
            copy.wait_recv()

    def rows_at(first):
        return pl.ds(pl.multiple_of(first, 16), block)

    def send_coded(stage, part, bit, blocks, source):
        @pl.loop(0, blocks)
        def _(i):
            code, unit = encode(source(i))
            code_to[stage][part, rows_at(i * block)] = code
            unit_to[stage][part, i] = unit

        send(
            [
                (code_to[stage].at[part], code_in[stage].at[part]),
                (unit_to[stage].at[part], unit_in[stage].at[part]),
            ],
            stage,
            part,
            bit,
        )

    def send_sum(step, part, bit, first, blocks):
        rows = pl.ds(pl.multiple_of(part * part_rows + first * block, 16), blocks * block)
        code_span = code_out.at[rows, mine]
        unit_span = unit_out.at[side, pl.ds(part * part_blocks + first, blocks)]
        send([(code_span, code_span), (unit_span, unit_span)], step, part, bit)

    def travel(p):
        start = p * part_rows
        send_coded(0, p, pair, part_blocks, lambda i: terms_ref[rows_at(start + i * block), other])
        yield
        base = 0
        for stage in range(stages):
            blocks = part_blocks >> stage
            arrived(p)

            @pl.loop(0, blocks)
            def _(i):
                value = decode(code_in[stage][p, rows_at(i * block)], unit_in[stage][p, i])
                if stage == 0:
                    own = terms_ref[rows_at(start + i * block), mine]
                else:
                    own = acc[p, rows_at((base + i) * block)]
                acc[p, rows_at((base + i) * block)] = own + value

            if stage < stages - 1:
                bit = orders[p][stage]
                half = blocks // 2
                away = base + (1 - bit_of(bit)) * half
                base = base + bit_of(bit) * half
                send_coded(stage + 1, p, bit, half, lambda i: acc[p, rows_at((away + i) * block)])
            else:
                code, unit = encode(acc[p, rows_at(base * block)] * scale)
                code_out[rows_at(start + base * block), mine] = code
                unit_out[side, p * part_blocks + base] = unit
                send_sum(stages, p, orders[p][-1], base, 1)
            yield
        for level in range(stages - 2, -1, -1):
            arrived(p)
            blocks = part_blocks >> level
            base = base - bit_of(orders[p][level]) * (blocks // 2)
            bit = orders[p][level - 1] if level > 0 else pair
            send_sum(2 * stages - 1 - level, p, bit, base, blocks)
            yield
        arrived(p)
        yield

    build_back = (lambda: build_center(1), lambda: build_edges(1))
    work = units(accs, ((), build_back))
    ways = [travel(p) for p in range(PARTS)]
    for p in range(PARTS):
        grad_terms(p, terms_ref)
        next(ways[p])
        if p > 0:
            next(ways[p - 1])
    next(ways[PARTS - 1])
    for event, p in enumerate(EVENTS):
        for _ in range(2 if event in DOUBLE else 1):
            next(work, None)
        next(ways[p])
    for way in ways:
        for _ in way:
            pass
    for _ in work:
        pass
    for copy in started:
        copy.wait_send()
    for slot, step in enumerate(HALO):
        @pl.when(inside(-1, step))
        def _():
            halo_copy(slot, -1)[1].wait_send()


def sum_plan(mesh, rows):
    sizes = dict(mesh.shape)
    if sizes["gx"] != 8 or sizes["gy"] != 4 or rows % (PARTS * 16 * 16):
        return None
    pair, x, y, z_near, z_far = ("gy", 1), ("gy", 2), ("gx", 1), ("gx", 2), ("gx", 4)
    return pair, [[z_near, z_far, x, y], [x, y, z_near, z_far], [y, x, z_near, z_far]]


def conv(plan, slots, scale, *operands):
    weights = operands[-2]
    width = weights.shape[-1]
    rows = slots * 512
    offsets = weights.shape[0]
    vmem = pl.BlockSpec(memory_space=VMEM)
    outs = [jax.ShapeDtypeStruct((rows, width), jnp.bfloat16)] * 2
    accs = [VMEM((rows, width), jnp.float32)] * 2
    full = (offsets * width, width)
    if plan is None:
        outs = outs + [jax.ShapeDtypeStruct(full, jnp.float32)]
        scratch = accs
        params = pltpu.CompilerParams(vmem_limit_bytes=58 * 2**20)
    else:
        stages = len(plan[1][0]) + 1
        part_rows = offsets * width // PARTS
        part_blocks = 1 << (stages - 1)
        outs = outs + [
            jax.ShapeDtypeStruct(full, jnp.int16),
            jax.ShapeDtypeStruct((2, PARTS * part_blocks, 1, LANES), jnp.float32),
        ]
        codes = [VMEM((PARTS, part_rows >> s, LANES), jnp.int16) for s in range(stages)]
        units = [VMEM((PARTS, part_blocks >> s, 1, LANES), jnp.float32) for s in range(stages)]
        sems = pltpu.SemaphoreType.DMA((2 * stages, PARTS, 2))
        scratch = (
            [VMEM(full, jnp.float32), VMEM((PARTS, part_rows, LANES), jnp.float32)]
            + accs
            + codes
            + codes
            + units
            + units
            + [sems, sems]
            + [VMEM((3, 2, slots, 10, wide, width), jnp.bfloat16) for wide in (80, 64)]
            + [VMEM((2, 2, slots, 64, width), jnp.bfloat16)] * 2
            + [VMEM((2, 2, 2, slots, 16, width), jnp.bfloat16)]
            + [VMEM((3, 2, 8, 8, width), jnp.float32)]
            + [pltpu.SemaphoreType.DMA((8,))] * 2
        )
        params = pltpu.CompilerParams(
            collective_id=0, has_side_effects=True, vmem_limit_bytes=58 * 2**20
        )
    return pl.pallas_call(
        functools.partial(conv_kernel, plan, slots, scale),
        in_specs=[vmem] * len(operands),
        out_specs=[vmem] * len(outs),
        out_shape=outs,
        scratch_shapes=scratch,
        compiler_params=params,
        cost_estimate=pl.CostEstimate(
            flops=offsets * 6 * rows * width * width, bytes_accessed=24 * 2**20, transcendentals=0
        ),
    )(*operands)


def finish_kernel(code_ref, unit_ref, feature_ref, grad_ref, mask_ref, sum_ref, feature_out, grad_out):
    for source, target in ((feature_ref, feature_out), (grad_ref, grad_out)):
        target[...] = (source[...].astype(jnp.float32) * mask_ref[...]).astype(target.dtype)
    steps = unit_ref.shape[1]
    block = code_ref.shape[0] // steps
    for i in range(steps):
        for side in range(2):
            at = slice(i * block, (i + 1) * block), slice(side * LANES, (side + 1) * LANES)
            sum_ref[at] = decode(code_ref[at], unit_ref[side, i])


def finish(code, unit, out, back, mask):
    rows, width = code.shape
    steps = 8
    tile = pl.BlockSpec((rows // steps, width), lambda i: (i, 0))
    voxels = pl.BlockSpec((out.shape[0] // steps, width), lambda i: (i, 0))
    flags = pl.BlockSpec((out.shape[0] // steps, 1), lambda i: (i, 0))
    units = pl.BlockSpec((2, unit.shape[1] // steps, 1, LANES), lambda i: (0, i, 0, 0))
    return pl.pallas_call(
        finish_kernel,
        grid=(steps,),
        in_specs=[tile, units, voxels, voxels, flags],
        out_specs=[tile, voxels, voxels],
        out_shape=[
            jax.ShapeDtypeStruct(code.shape, jnp.float32),
            jax.ShapeDtypeStruct(out.shape, out.dtype),
            jax.ShapeDtypeStruct(back.shape, back.dtype),
        ],
        compiler_params=pltpu.CompilerParams(vmem_limit_bytes=24 * 2**20),
        cost_estimate=pl.CostEstimate(
            flops=2 * rows * width, bytes_accessed=8 * rows * width, transcendentals=0
        ),
    )(code, unit, out, back, mask)


def shards(plan, features, cotangent, kernel, occupancy, neighbors):
    slots = features.shape[0]
    width = features.shape[-1]
    mask_b = occupancy.reshape(slots, 8, 8, 8, 1).astype(jnp.bfloat16)
    masked = features * mask_b
    masked_grad = cotangent * mask_b
    both = jnp.stack([masked, masked_grad])
    grad_t = masked_grad.reshape(-1, width).T
    scale = 1.0 / (512.0 * slots * lax.axis_size("gx") * lax.axis_size("gy")) ** 0.5
    if width != 2 * LANES:
        plan = None
    if plan is None:
        shifted = z_shifted(both, neighbors)
        even = shifted.reshape(3, 2, slots, 10, 80, width)
        odd = shifted[:, :, :, :, 1:9].reshape(3, 2, slots, 10, 64, width)
        operands = even, odd
    else:
        sides = jnp.stack([both[:, :, :, 0], both[:, :, :, 7]])
        corners = jnp.stack([sides[:, :, :, 0], sides[:, :, :, 7]])
        corners = jnp.concatenate([corners, jnp.zeros_like(corners)], -2)
        near = jnp.broadcast_to(neighbors.reshape(-1, 1, 1), (neighbors.size, 1, width))
        operands = both.reshape(2, slots, 8, 64, width), sides.reshape(2, 2, slots, 64, width), corners, near
    out, back, *total = conv(plan, slots, scale, *operands, kernel, grad_t)
    if plan is None:
        kernel_grad = lax.psum(total[0], ("gx", "gy")) * jnp.float32(scale)
        flat_mask = mask_b.reshape(-1, 1)
        out, back = out * flat_mask, back * flat_mask
    else:
        mask = occupancy.reshape(-1, 1).astype(jnp.float32)
        kernel_grad, out, back = finish(*total, out, back, mask)
    return (
        out.reshape(features.shape),
        back.reshape(features.shape),
        kernel_grad.reshape(kernel.shape),
    )


def solution(mesh):
    placed = (
        P(("gx", "gy"), None, None, None, None),
        P(("gx", "gy"), None, None, None, None),
        P(),
        P(("gx", "gy"), None),
        P(("gx", "gy"), None),
    )
    plan = sum_plan(mesh, 27 * 256)
    return jax.shard_map(
        functools.partial(shards, plan),
        mesh=mesh,
        in_specs=placed,
        out_specs=(
            P(("gx", "gy"), None, None, None, None),
            P(("gx", "gy"), None, None, None, None),
            P(),
        ),
        check_vma=False,
    )
```

```python
import functools

import jax
import jax.numpy as jnp
from jax import lax
from jax.experimental import pallas as pl
from jax.experimental.pallas import tpu as pltpu
from jax.sharding import PartitionSpec as P

MESH = pl.DeviceIdType.MESH
VMEM = pltpu.VMEM
PARTS = 3
LANES = 128
HALO = ((-1, 0), (1, 0), (0, -1), (0, 1), (-1, -1), (-1, 1), (1, -1), (1, 1))
UNITS_AFTER = (2, 2, 1, 0)
UNITS_BACK = (0, 1, 1, 0)


def shift_by_one(cells, axis):
    count = lax.axis_size(axis)
    ends = count - 1
    head = lambda dim: lax.slice_in_dim(cells, 0, 1, axis=dim)
    tail = lambda dim: lax.slice_in_dim(cells, cells.shape[dim] - 1, cells.shape[dim], axis=dim)
    up = [(i, i + 1) for i in range(ends)]
    down = [(i + 1, i) for i in range(ends)]
    return lambda dim: jnp.concatenate(
        [lax.ppermute(tail(dim), axis, up), cells, lax.ppermute(head(dim), axis, down)], axis=dim
    )


def spread(table, dim):
    first = lax.slice_in_dim(table, 0, 1, axis=dim)
    middle = lax.slice_in_dim(table, 1, 2, axis=dim)
    last = lax.slice_in_dim(table, 2, 3, axis=dim)
    return jnp.concatenate([first] + [middle] * 8 + [last], axis=dim)


def z_shifted(both, neighbors):
    slots = both.shape[1]
    wide = shift_by_one(both, "gx")(2)
    wide = shift_by_one(wide, "gy")(3)
    table = spread(spread(neighbors.reshape(slots, 3, 3, 3), 1), 2)

    def pick(layer, oz):
        total = None
        for slot in range(slots):
            hit = (table[:, :, :, oz] == slot)[None, :, :, :, None, None]
            part = jnp.where(hit, wide[:, slot : slot + 1, :, :, layer], jnp.zeros((), wide.dtype))
            total = part if total is None else total + part
        return total

    low = pick(slice(7, 8), 0)
    mid = pick(slice(0, 8), 1)
    high = pick(slice(0, 1), 2)
    return jnp.stack(
        [
            jnp.concatenate([low, mid[..., :7, :]], 4),
            mid,
            jnp.concatenate([mid[..., 1:, :], high], 4),
        ]
    )


def encode(values):
    peak = jnp.maximum(jnp.max(jnp.abs(values), axis=0, keepdims=True), 1e-33)
    return jnp.round(values * (32767.0 / peak)).astype(jnp.int32).astype(jnp.int16), peak * (1.0 / 32767.0)


def decode(code, unit):
    return code.astype(jnp.int32).astype(jnp.float32) * unit


def conv_kernel(plan, slots, scale, *refs):
    if plan is None:
        even_ref, odd_ref, w_ref, grad_t_ref, out_ref, back_ref, *rest = refs
    else:
        both_ref, y_ref, corner_ref, near_ref, w_ref, grad_t_ref, out_ref, back_ref, *rest = refs
    width = w_ref.shape[-1]

    def window(tensor, brick, ox, oy, oz):
        if oy == 1:
            value = odd_ref[oz, tensor, brick, ox : ox + 8]
        else:
            value = even_ref[oz, tensor, brick, ox : ox + 8, 8 * oy : 8 * oy + 64]
        return value.reshape(512, width)

    def grad_terms(ox, terms_ref):
        for oy in range(3):
            for oz in range(3):
                both = jnp.concatenate([window(0, brick, ox, oy, oz) for brick in range(slots)], 0)
                term = jnp.dot(grad_t_ref[...], both, preferred_element_type=jnp.float32)
                offset = 9 * ox + 3 * oy + oz
                terms_ref[offset * width : (offset + 1) * width] = term.T

    def features_unit(tensor, ox, acc):
        for oy in range(3):
            first = 9 * ox + 3 * oy
            if tensor == 0:
                rhs = w_ref[first : first + 3].reshape(3 * width, width)
            else:
                rhs = jnp.concatenate([w_ref[26 - first - oz] for oz in range(3)], 1)
            for brick in range(slots):
                rows = slice(512 * brick, 512 * brick + 512)
                lhs = jnp.concatenate([window(tensor, brick, ox, oy, oz) for oz in range(3)], 1)
                part = lax.dot_general(
                    lhs, rhs, (((1,), (tensor,)), ((), ())), preferred_element_type=jnp.float32
                )
                if ox == 0 and oy == 0:
                    acc[rows] = part
                else:
                    acc[rows] += part

    def units(accs, prepare):
        for tensor, acc, target in ((0, accs[0], out_ref), (1, accs[1], back_ref)):
            if tensor == 1:
                prepare()
                yield
            for ox in range(3):
                features_unit(tensor, ox, acc)
                if ox == 2:
                    target[...] = acc[...].astype(target.dtype)
                yield

    if plan is None:
        terms_ref, *accs = rest
        for ox in range(3):
            grad_terms(ox, terms_ref)
        for _ in units(accs, lambda: None):
            pass
        return

    pair, orders = plan
    stages = len(orders[0]) + 1
    code_out, unit_out, terms_ref, acc, *accs = rest[:6]
    buffers = rest[6 : 6 + 4 * stages]
    code_to, code_in, unit_to, unit_in = (buffers[i * stages : (i + 1) * stages] for i in range(4))
    send_sem, recv_sem, even_ref, odd_ref, *halo = rest[6 + 4 * stages :]
    halo_x, halo_y, halo_corner, edge_y, halo_send, halo_recv = halo
    part_rows = acc.shape[1]
    block = part_rows >> (stages - 1)
    part_blocks = part_rows // block
    place = {"gx": lax.axis_index("gx"), "gy": lax.axis_index("gy")}

    def bit_of(bit):
        axis, step = bit
        return (place[axis] // step) % 2

    def partner(bit):
        axis, step = bit
        there = dict(place)
        there[axis] = place[axis] + step - 2 * step * bit_of(bit)
        return (there["gx"], there["gy"])

    barrier = pltpu.get_barrier_semaphore()
    for bit in [pair] + sorted(orders[0]):
        pl.semaphore_signal(barrier, inc=1, device_id=partner(bit), device_id_type=MESH)

    def inside(sign, step):
        col_x, col_y = place["gx"] + sign * step[0], place["gy"] + sign * step[1]
        x_in = (col_x >= 0) & (col_x < lax.axis_size("gx"))
        return x_in & (col_y >= 0) & (col_y < lax.axis_size("gy"))

    def halo_copy(slot, sign):
        step = HALO[slot]
        low_x, low_y = int(step[0] > 0), int(step[1] > 0)
        if step[1] == 0:
            src, dst = both_ref.at[:, :, 0 if low_x else 7], halo_x.at[low_x]
        elif step[0] == 0:
            src, dst = y_ref.at[1 - low_y], halo_y.at[low_y]
        else:
            src, dst = corner_ref.at[1 - low_x, 1 - low_y], halo_corner.at[low_x, low_y]
        there = (place["gx"] + sign * step[0], place["gy"] + sign * step[1])
        return dst, pltpu.make_async_remote_copy(
            src_ref=src,
            dst_ref=dst,
            send_sem=halo_send.at[slot],
            recv_sem=halo_recv.at[slot],
            device_id=there,
            device_id_type=MESH,
        )

    near = stages
    for slot, step in enumerate(HALO):
        near = near + inside(1, step).astype(jnp.int32)

        @pl.when(inside(-1, step))
        def _():
            there = (place["gx"] - step[0], place["gy"] - step[1])
            pl.semaphore_signal(barrier, inc=1, device_id=there, device_id_type=MESH)

    pl.semaphore_wait(barrier, near)
    for slot, step in enumerate(HALO):
        @pl.when(inside(-1, step))
        def _():
            halo_copy(slot, -1)[1].start()

    height = lax.broadcasted_iota(jnp.int32, (1, 8, width), 1)

    def extended_z(sources, brick, first):
        def pick(offset):
            slot_row = near_ref[brick * 27 + first + offset]
            total = jnp.zeros_like(sources[0])
            for slot in range(slots):
                total = jnp.where(slot_row[None] == slot, sources[slot], total)
            return total

        low, mid, high = pick(0), pick(1), pick(2)
        return [
            pltpu.roll(jnp.where(height == 7, low, mid), 1, 1),
            mid,
            pltpu.roll(jnp.where(height == 0, high, mid), 7, 1),
        ]

    def cells(value):
        return value.astype(jnp.float32).reshape(-1, 8, width)

    def rows_of(value):
        return value.reshape(-1, width).astype(jnp.bfloat16)

    def build_center(tensor):
        @pl.loop(0, slots)
        def _(brick):

            @pl.loop(0, 8)
            def _(x):
                sources = [cells(both_ref[tensor, slot, x]) for slot in range(slots)]
                for oz, value in enumerate(extended_z(sources, brick, 12)):
                    odd_ref[oz, tensor, brick, x + 1] = rows_of(value)

    def build_edges(tensor):
        @pl.loop(0, slots)
        def _(brick):
            for end in range(2):
                sources = [cells(halo_y[end, tensor, slot]) for slot in range(slots)]
                for oz, value in enumerate(extended_z(sources, brick, 9 + 6 * end)):
                    edge_y[oz, end] = value

            @pl.loop(0, 8)
            def _(x):
                for oz in range(3):
                    middle = cells(odd_ref[oz, tensor, brick, x + 1])
                    row = jnp.concatenate([edge_y[oz, 0, pl.ds(x, 1)], middle, edge_y[oz, 1, pl.ds(x, 1)]], 0)
                    even_ref[oz, tensor, brick, x + 1] = rows_of(row)

            for end in range(2):
                first = 18 * end
                middle = extended_z(
                    [cells(halo_x[end, tensor, slot]) for slot in range(slots)], brick, first + 3
                )
                ends = []
                for end_y in range(2):
                    column = [
                        halo_corner[end, end_y, tensor, slot].astype(jnp.float32)[None, :8]
                        for slot in range(slots)
                    ]
                    ends.append(extended_z(column, brick, first + 6 * end_y))
                for oz in range(3):
                    row = jnp.concatenate([ends[0][oz], middle[oz], ends[1][oz]], 0)
                    even_ref[oz, tensor, brick, 9 * end] = rows_of(row)
                    odd_ref[oz, tensor, brick, 9 * end] = rows_of(middle[oz])

    build_center(0)
    for slot, step in enumerate(HALO):
        dst, arriving = halo_copy(slot, 1)

        @pl.when(inside(1, step))
        def _():
            arriving.wait_recv()

        @pl.when(jnp.logical_not(inside(1, step)))
        def _():
            dst[...] = jnp.zeros(dst.shape, dst.dtype)

    build_edges(0)
    side = bit_of(pair)
    mine = pl.ds(pl.multiple_of(side * LANES, LANES), LANES)
    other = pl.ds(pl.multiple_of((1 - side) * LANES, LANES), LANES)
    started = []
    flying = [None] * PARTS

    def send(spans, step, part, bit):
        flying[part] = []
        for which, (src, dst) in enumerate(spans):
            copy = pltpu.make_async_remote_copy(
                src_ref=src,
                dst_ref=dst,
                send_sem=send_sem.at[step, part, which],
                recv_sem=recv_sem.at[step, part, which],
                device_id=partner(bit),
                device_id_type=MESH,
            )
            copy.start()
            started.append(copy)
            flying[part].append(copy)

    def arrived(part):
        for copy in flying[part]:
            copy.wait_recv()

    def rows_at(first):
        return pl.ds(pl.multiple_of(first, 16), block)

    def send_coded(stage, part, bit):
        send(
            [
                (code_to[stage].at[part], code_in[stage].at[part]),
                (unit_to[stage].at[part], unit_in[stage].at[part]),
            ],
            stage,
            part,
            bit,
        )

    def build_back():
        build_center(1)
        build_edges(1)

    work = units(accs, build_back)
    base = [0] * PARTS
    for p in range(PARTS):
        grad_terms(p, terms_ref)

        @pl.loop(0, part_blocks)
        def _(i):
            code, unit = encode(terms_ref[rows_at(p * part_rows + i * block), other])
            code_to[0][p, rows_at(i * block)] = code
            unit_to[0][p, i] = unit

        send_coded(0, p, pair)

    for stage in range(stages):
        blocks = part_blocks >> stage
        for p in range(PARTS):
            arrived(p)

            @pl.loop(0, blocks)
            def _(i):
                value = decode(code_in[stage][p, rows_at(i * block)], unit_in[stage][p, i])
                if stage == 0:
                    own = terms_ref[rows_at(p * part_rows + i * block), mine]
                else:
                    own = acc[p, rows_at((base[p] + i) * block)]
                acc[p, rows_at((base[p] + i) * block)] = own + value

            if stage < stages - 1:
                bit = orders[p][stage]
                half = blocks // 2
                away = base[p] + (1 - bit_of(bit)) * half
                base[p] = base[p] + bit_of(bit) * half

                @pl.loop(0, half)
                def _(i):
                    code, unit = encode(acc[p, rows_at((away + i) * block)])
                    code_to[stage + 1][p, rows_at(i * block)] = code
                    unit_to[stage + 1][p, i] = unit

                send_coded(stage + 1, p, bit)
            else:
                code, unit = encode(acc[p, rows_at(base[p] * block)] * scale)
                code_out[rows_at(p * part_rows + base[p] * block), mine] = code
                unit_out[side, p * part_blocks + base[p]] = unit
        for _ in range(UNITS_AFTER[stage] if stage < stages - 1 else 0):
            next(work, None)
        if stage < stages - 1:
            continue
        for p in range(PARTS):
            code_span = code_out.at[rows_at(p * part_rows + base[p] * block), mine]
            unit_span = unit_out.at[side, pl.ds(p * part_blocks + base[p], 1)]
            send([(code_span, code_span), (unit_span, unit_span)], stages, p, orders[p][-1])

    for back in range(1, stages + 1):
        level = stages - 1 - back
        for p in range(PARTS):
            arrived(p)
            if level < 0:
                continue
            blocks = part_blocks >> level
            base[p] = base[p] - bit_of(orders[p][level]) * (blocks // 2)
            first = pl.multiple_of(p * part_rows + base[p] * block, 16)
            code_span = code_out.at[pl.ds(first, blocks * block), mine]
            unit_span = unit_out.at[side, pl.ds(p * part_blocks + base[p], blocks)]
            bit = orders[p][level - 1] if level > 0 else pair
            send([(code_span, code_span), (unit_span, unit_span)], stages + back, p, bit)
        if level >= 0:
            for _ in range(UNITS_BACK[back - 1]):
                next(work, None)
    for _ in work:
        pass
    for copy in started:
        copy.wait_send()
    for slot, step in enumerate(HALO):
        @pl.when(inside(-1, step))
        def _():
            halo_copy(slot, -1)[1].wait_send()


def sum_plan(mesh, rows):
    sizes = dict(mesh.shape)
    if sizes["gx"] != 8 or sizes["gy"] != 4 or rows % (PARTS * 16 * 16):
        return None
    pair, x, y, z_near, z_far = ("gy", 1), ("gy", 2), ("gx", 1), ("gx", 2), ("gx", 4)
    return pair, [[x, y, z_near, z_far], [y, x, z_near, z_far], [z_near, z_far, x, y]]


def conv(plan, slots, scale, *operands):
    weights = operands[-2]
    width = weights.shape[-1]
    rows = slots * 512
    offsets = weights.shape[0]
    vmem = pl.BlockSpec(memory_space=VMEM)
    outs = [jax.ShapeDtypeStruct((rows, width), jnp.bfloat16)] * 2
    accs = [VMEM((rows, width), jnp.float32)] * 2
    full = (offsets * width, width)
    if plan is None:
        outs = outs + [jax.ShapeDtypeStruct(full, jnp.float32)]
        scratch = accs
        params = pltpu.CompilerParams(vmem_limit_bytes=58 * 2**20)
    else:
        stages = len(plan[1][0]) + 1
        part_rows = offsets * width // PARTS
        part_blocks = 1 << (stages - 1)
        outs = outs + [
            jax.ShapeDtypeStruct(full, jnp.int16),
            jax.ShapeDtypeStruct((2, PARTS * part_blocks, 1, LANES), jnp.float32),
        ]
        codes = [VMEM((PARTS, part_rows >> s, LANES), jnp.int16) for s in range(stages)]
        units = [VMEM((PARTS, part_blocks >> s, 1, LANES), jnp.float32) for s in range(stages)]
        sems = pltpu.SemaphoreType.DMA((2 * stages, PARTS, 2))
        scratch = (
            [VMEM(full, jnp.float32), VMEM((PARTS, part_rows, LANES), jnp.float32)]
            + accs
            + codes
            + codes
            + units
            + units
            + [sems, sems]
            + [VMEM((3, 2, slots, 10, wide, width), jnp.bfloat16) for wide in (80, 64)]
            + [VMEM((2, 2, slots, 64, width), jnp.bfloat16)] * 2
            + [VMEM((2, 2, 2, slots, 16, width), jnp.bfloat16)]
            + [VMEM((3, 2, 8, 8, width), jnp.float32)]
            + [pltpu.SemaphoreType.DMA((8,))] * 2
        )
        params = pltpu.CompilerParams(
            collective_id=0, has_side_effects=True, vmem_limit_bytes=58 * 2**20
        )
    return pl.pallas_call(
        functools.partial(conv_kernel, plan, slots, scale),
        in_specs=[vmem] * len(operands),
        out_specs=[vmem] * len(outs),
        out_shape=outs,
        scratch_shapes=scratch,
        compiler_params=params,
        cost_estimate=pl.CostEstimate(
            flops=offsets * 6 * rows * width * width, bytes_accessed=24 * 2**20, transcendentals=0
        ),
    )(*operands)


def finish_kernel(code_ref, unit_ref, feature_ref, grad_ref, mask_ref, sum_ref, feature_out, grad_out):
    for source, target in ((feature_ref, feature_out), (grad_ref, grad_out)):
        target[...] = (source[...].astype(jnp.float32) * mask_ref[...]).astype(target.dtype)
    steps = unit_ref.shape[1]
    block = code_ref.shape[0] // steps
    for i in range(steps):
        for side in range(2):
            at = slice(i * block, (i + 1) * block), slice(side * LANES, (side + 1) * LANES)
            sum_ref[at] = decode(code_ref[at], unit_ref[side, i])


def finish(code, unit, out, back, mask):
    rows, width = code.shape
    steps = 8
    tile = pl.BlockSpec((rows // steps, width), lambda i: (i, 0))
    voxels = pl.BlockSpec((out.shape[0] // steps, width), lambda i: (i, 0))
    flags = pl.BlockSpec((out.shape[0] // steps, 1), lambda i: (i, 0))
    units = pl.BlockSpec((2, unit.shape[1] // steps, 1, LANES), lambda i: (0, i, 0, 0))
    return pl.pallas_call(
        finish_kernel,
        grid=(steps,),
        in_specs=[tile, units, voxels, voxels, flags],
        out_specs=[tile, voxels, voxels],
        out_shape=[
            jax.ShapeDtypeStruct(code.shape, jnp.float32),
            jax.ShapeDtypeStruct(out.shape, out.dtype),
            jax.ShapeDtypeStruct(back.shape, back.dtype),
        ],
        compiler_params=pltpu.CompilerParams(vmem_limit_bytes=58 * 2**20),
        cost_estimate=pl.CostEstimate(
            flops=2 * rows * width, bytes_accessed=8 * rows * width, transcendentals=0
        ),
    )(code, unit, out, back, mask)


def shards(plan, features, cotangent, kernel, occupancy, neighbors):
    slots = features.shape[0]
    width = features.shape[-1]
    mask_b = occupancy.reshape(slots, 8, 8, 8, 1).astype(jnp.bfloat16)
    masked = features * mask_b
    masked_grad = cotangent * mask_b
    both = jnp.stack([masked, masked_grad])
    grad_t = masked_grad.reshape(-1, width).T
    scale = 1.0 / (512.0 * slots * lax.axis_size("gx") * lax.axis_size("gy")) ** 0.5
    if width != 2 * LANES:
        plan = None
    if plan is None:
        shifted = z_shifted(both, neighbors)
        even = shifted.reshape(3, 2, slots, 10, 80, width)
        odd = shifted[:, :, :, :, 1:9].reshape(3, 2, slots, 10, 64, width)
        operands = even, odd
    else:
        sides = jnp.stack([both[:, :, :, 0], both[:, :, :, 7]])
        corners = jnp.stack([sides[:, :, :, 0], sides[:, :, :, 7]])
        corners = jnp.concatenate([corners, jnp.zeros_like(corners)], -2)
        near = jnp.broadcast_to(neighbors.reshape(-1, 1, 1), (neighbors.size, 1, width))
        operands = both.reshape(2, slots, 8, 64, width), sides.reshape(2, 2, slots, 64, width), corners, near
    out, back, *total = conv(plan, slots, scale, *operands, kernel, grad_t)
    if plan is None:
        kernel_grad = lax.psum(total[0], ("gx", "gy")) * jnp.float32(scale)
        flat_mask = mask_b.reshape(-1, 1)
        out, back = out * flat_mask, back * flat_mask
    else:
        mask = occupancy.reshape(-1, 1).astype(jnp.float32)
        kernel_grad, out, back = finish(*total, out, back, mask)
    return (
        out.reshape(features.shape),
        back.reshape(features.shape),
        kernel_grad.reshape(kernel.shape),
    )


def solution(mesh):
    placed = (
        P(("gx", "gy"), None, None, None, None),
        P(("gx", "gy"), None, None, None, None),
        P(),
        P(("gx", "gy"), None),
        P(("gx", "gy"), None),
    )
    plan = sum_plan(mesh, 27 * 256)
    return jax.shard_map(
        functools.partial(shards, plan),
        mesh=mesh,
        in_specs=placed,
        out_specs=(
            P(("gx", "gy"), None, None, None, None),
            P(("gx", "gy"), None, None, None, None),
            P(),
        ),
        check_vma=False,
    )
```
